256 devices in a mesh: layer: 16 (over x, y), dp: 4 (over z_lo, core), tensor: 4 (over z_hi).
Axes of the slice: x: 4, y: 4, z: 8 (z_hi: 4, z_lo: 2; z = z_hi * 2 + z_lo), core: 2. Of those that a mesh axis runs over, the one named last changes fastest.
Arguments:
- hidden: bfloat16 [2, 16384, 8192], P(None, ('layer', 'dp'), 'tensor'), may hold values from -60 to 60
- queries: bfloat16 [2, 16384, 4096], P(None, ('layer', 'dp'), 'tensor'), may hold values from -70 to 70
- cotangent: bfloat16 [2, 16384, 4096], P(None, ('layer', 'dp'), 'tensor'), may hold values from -6 to 6
- slabs: bfloat16 [2, 8192, 1024], P(None, 'layer', 'tensor'), may hold values from -0.0625 to 0.0625
Outputs:
- attended: bfloat16 [2, 16384, 4096], P(None, ('layer', 'dp'), 'tensor')
- query_grads: bfloat16 [2, 16384, 4096], P(None, ('layer', 'dp'), 'tensor')
- hidden_grads: bfloat16 [2, 16384, 8192], P(None, ('layer', 'dp'), 'tensor')
- slab_grads: float32 [2, 8192, 1024], P(None, 'layer', 'tensor')
The draws below stay inside these ranges and needn't reach their ends.
All inputs are finite; a program needn't handle non-finite values.
Results may differ from the reference program's by a relative error of at most 0.025.
The reference program's roundings to bfloat16 on the way (of `normed`, `projected`, `weights` and `joined`) count: a program that leaves them out, or rounds other values in their place, can miss the bound.
Values may be sent and summed in bfloat16 or wider, within the bound.
No kernel may reach another device: no remote copies, remote signals or barrier semaphores. Data moves between devices by JAX's collectives and lax.ppermute only.
A program may use at most 128 MiB of HBM per device.

```python
import jax
import jax.numpy as jnp
from jax import lax

D = 8192
HD = 128
KVH = 4
GROUP = 8
SEQ_LEN = 256
TOK_DEV = 256
TOKENS = 16384
QH = 32


def feature_scales(top_scale):
    position = jnp.arange(D, dtype=jnp.float32) / (D - 1)
    return jnp.exp(position * jnp.log(jnp.float32(top_scale)))


def draw_hidden(key, part):
    key = jax.random.fold_in(key, 11)
    array_shape = (2, TOKENS, D)
    values = jnp.clip(jax.random.normal(key, array_shape, jnp.float32), -6.0, 6.0)
    return (values * feature_scales(10.0)).astype(jnp.bfloat16)


def draw_queries(key, part):
    key = jax.random.fold_in(key, 7)
    array_shape = (2, TOKENS, KVH * GROUP * HD)
    first_key = jax.random.fold_in(key, 0)
    return jnp.clip(jax.random.normal(first_key, array_shape, jnp.float32), -4.0, 4.0).astype(jnp.bfloat16)


def levels(rng, shape, cuts, smallest, top_value):
    def one(dim, parts):
        steps = jax.random.uniform(jax.random.fold_in(jax.random.fold_in(rng, 6), dim), (parts,), jnp.float32, smallest / len(cuts), top_value / len(cuts))
        return jnp.repeat(jnp.exp(steps), shape[dim] // parts).reshape((-1,) + (1,) * (len(shape) - dim - 1))

    gain = one(*cuts[0])
    for cut in cuts[1:]:
        gain = gain * one(*cut)
    return gain


def bell_draw(stream_key, extent, deviation, most, cuts=(), held_as=jnp.bfloat16):
    values = jax.random.normal(stream_key, extent, jnp.float32) * deviation
    if len(cuts) > 0:
        values = levels(stream_key, extent, cuts, -0.22, 0.18) * values
    return jnp.clip(values, min=-most, max=most).astype(held_as)


def setup_inputs(seed: int = 0) -> dict:
    streams_of = jax.random.split(jax.random.key(seed), 5)
    hidden = draw_hidden(jax.random.fold_in(streams_of[4], 71), 0)
    queries = draw_queries(jax.random.fold_in(streams_of[4], 71), 0)
    cotangent = bell_draw(streams_of[2], (2, TOKENS, QH * HD), 1.0, 6.0, ((1, 64), (2, 4)))
    slabs = bell_draw(streams_of[3], (2, D, KVH * 2 * HD), D ** -0.5, 0.0625, ((1, 16), (2, 4)))
    return dict(hidden=hidden, queries=queries, cotangent=cotangent, slabs=slabs)


EPSILON = 1e-05

def attend(query_rows, key_rows, value_rows):
    scores = jnp.einsum('slhge,smhe->shglm', query_rows.astype(jnp.float32), key_rows.astype(jnp.float32))
    scores = scores * query_rows.shape[-1] ** (-0.5)
    length = query_rows.shape[1]
    position = jnp.arange(length)
    causal = position[:, None] >= position[None, :]
    scores = jnp.where(causal, scores, -1e+30)
    highest = lax.optimization_barrier(jnp.max(scores, axis=-1, keepdims=True))
    weights = jnp.exp(scores - highest)
    weights = (weights / lax.optimization_barrier(jnp.sum(weights, axis=-1, keepdims=True))).astype(jnp.bfloat16)
    mixed_rows = jnp.einsum('shglm,smhe->slhge', weights.astype(jnp.float32), value_rows.astype(jnp.float32))
    return mixed_rows.astype(jnp.bfloat16)

def normalize(state_rows):
    floats = state_rows.astype(jnp.float32)
    inverse = lax.rsqrt(lax.optimization_barrier(jnp.mean(floats * floats, axis=-1, keepdims=True)) + EPSILON)
    return (floats * inverse, inverse)

def reference(hidden, queries, cotangent, slabs):
    seq_count = TOKENS // SEQ_LEN
    block_count = TOKENS // TOK_DEV
    column_count = KVH * 2 * HD
    attended_list = []
    query_list = []
    hidden_list = []
    slab_list = []
    for depth in range(2):
        scaled, inverse = normalize(hidden[depth])
        normed = scaled.astype(jnp.bfloat16)
        layer_slab = slabs[depth]
        projected = jnp.dot(normed, layer_slab, preferred_element_type=jnp.float32).astype(jnp.bfloat16)
        projected = projected.reshape(TOKENS, KVH, 2, HD)
        key_rows = projected[:, :, 0].reshape(seq_count, SEQ_LEN, KVH, HD)
        value_rows = projected[:, :, 1].reshape(seq_count, SEQ_LEN, KVH, HD)
        query_rows = queries[depth].reshape(seq_count, SEQ_LEN, KVH, GROUP, HD)
        output, pullback = jax.vjp(attend, query_rows, key_rows, value_rows)
        query_grad, key_grad, value_grad = pullback(cotangent[depth].reshape(seq_count, SEQ_LEN, KVH, GROUP, HD))
        joined = jnp.stack([key_grad.reshape(TOKENS, KVH, HD), value_grad.reshape(TOKENS, KVH, HD)], axis=2)
        joined = joined.reshape(TOKENS, column_count)

        def accumulate(running, block_pair):
            normed_block, joined_block = block_pair
            block_term = lax.dot_general(normed_block, joined_block, (((0,), (0,)), ((), ())), preferred_element_type=jnp.float32)
            return (running + lax.optimization_barrier(block_term.astype(jnp.bfloat16)).astype(jnp.float32), None)
        slab_grad, _ = lax.scan(accumulate, jnp.zeros((D, column_count), jnp.float32), (normed.reshape(block_count, TOK_DEV, D), joined.reshape(block_count, TOK_DEV, column_count)))
        spread = jnp.zeros((TOKENS, D), jnp.float32)
        for kv_head in range(KVH):
            first_col = kv_head * 2 * HD
            head_term = lax.dot_general(joined[:, first_col:first_col + 2 * HD], layer_slab[:, first_col:first_col + 2 * HD], (((1,), (1,)), ((), ())), preferred_element_type=jnp.float32)
            spread = spread + lax.optimization_barrier(head_term.astype(jnp.bfloat16)).astype(jnp.float32)
        products = lax.optimization_barrier(jnp.mean(spread * scaled, axis=-1, keepdims=True))
        input_grad = (inverse * (spread - scaled * products)).astype(jnp.bfloat16)
        attended_list.append(output.reshape(TOKENS, QH * HD))
        query_list.append(query_grad.reshape(TOKENS, QH * HD))
        hidden_list.append(input_grad)
        slab_list.append(slab_grad)
    return (jnp.stack(attended_list), jnp.stack(query_list), jnp.stack(hidden_list), jnp.stack(slab_list))
```

```python
import functools

import jax
import jax.numpy as jnp
from jax import lax
from jax.experimental import pallas as pl
from jax.experimental.pallas import tpu as pltpu
from jax.sharding import PartitionSpec as P

D = 8192
HD = 128
GROUP = 8
SEQ = 256
EPSILON = 1e-05
BF16 = jnp.bfloat16
F32 = jnp.float32
AXES = ("layer", "dp", "tensor")
BLOCK = 256
VMEM_BYTES = 40 * 1024 * 1024


def route(move):
    def flat(x, y, low, core, high):
        return ((x * 4 + y) * 4 + low * 2 + core) * 4 + high

    pairs = []
    for x in range(4):
        for y in range(4):
            for low in range(2):
                for core in range(2):
                    for high in range(4):
                        pairs.append((flat(x, y, low, core, high), flat(*move(x, y, low, core, high))))
    return pairs


def along(axis, step):
    if axis == "x":
        return route(lambda x, y, low, core, high: ((x + step) % 4, y, low, core, high))
    if axis == "y":
        return route(lambda x, y, low, core, high: (x, (y + step) % 4, low, core, high))
    return route(lambda x, y, low, core, high: (x, y, low, core, (high + step) % 4))


CORE = route(lambda x, y, low, core, high: (x, y, low, 1 - core, high))
LOW = route(lambda x, y, low, core, high: (x, y, 1 - low, core, high))
SWAP = route(lambda x, y, low, core, high: (high, y, low, core, x))


def shift(value, pairs):
    return lax.ppermute(value, AXES, pairs)


def gather(block, first, second):
    row = jnp.stack([block] + [shift(block, along(first, -k)) for k in (1, 2, 3)])
    return [row] + [shift(row, along(second, -k)) for k in (1, 2, 3)]


def scatter(rows, first, second):
    arrived = [shift(rows[k].astype(BF16), along(first, k)) for k in (1, 2, 3)]
    total = rows[0] + sum(part.astype(F32) for part in arrived)
    rounded = total.astype(BF16)
    arrived = [shift(rounded[k], along(second, k)) for k in (1, 2, 3)]
    return total[0] + sum(part.astype(F32) for part in arrived)


def piece(refs, x_inner, dx, dy):
    return refs[dy][dx] if x_inner else refs[dx][dy]


def dot(a, b, ca, cb):
    return lax.dot_general(a, b, (((ca,), (cb,)), ((), ())), preferred_element_type=F32)


def project_kernel(x_inner, where, hidden, inverse, *refs):
    mine, theirs = refs[:4], refs[4:8]
    normed, outs, total = refs[8], refs[9:13], refs[13]
    x, y, core, high = where[0], where[1], where[2], where[3]
    for chunk in range(8):
        part = hidden[0, :, chunk * BLOCK : (chunk + 1) * BLOCK].astype(F32) * inverse[0]
        normed[chunk] = part.astype(BF16)
    for dx in range(4):
        acc = jnp.zeros((SEQ, BLOCK), F32)
        for dy in range(4):
            row = lax.rem(y + dy, 4) * 2
            acc += dot(normed[row + core], piece(mine, x_inner, dx, dy), 1, 0)
            acc += dot(normed[row + 1 - core], piece(theirs, x_inner, dx, dy), 1, 0)
        total[lax.rem(x + dx, 4)] = acc
    for k in range(4):
        outs[k][...] = total[lax.rem(high + k, 4)]


def attend_kernel(has_old, *refs):
    parts, refs = refs[:4], refs[4:]
    query, cotangent = refs[:2]
    refs = refs[4:] if has_old else refs[2:]
    attended, query_grad, joined, keys, values, key_grad, value_grad = refs
    head = pl.program_id(0)

    @pl.when(head == 0)
    def _():
        projected = (parts[0][...] + parts[1][...]) + (parts[2][...] + parts[3][...])
        keys[...] = projected[:, :HD].astype(BF16)
        values[...] = projected[:, HD:].astype(BF16)
        key_grad[...] = jnp.zeros_like(key_grad)
        value_grad[...] = jnp.zeros_like(value_grad)

    q, out_grad = query[0], cotangent[0]
    k, v = keys[...], values[...]
    scores = dot(q, k, 1, 1) * HD**-0.5
    at = lax.broadcasted_iota(jnp.int32, (SEQ, SEQ), 0)
    to = lax.broadcasted_iota(jnp.int32, (SEQ, SEQ), 1)
    scores = jnp.where(at >= to, scores, -1e30)
    weights = jnp.exp(scores - jnp.max(scores, axis=-1, keepdims=True))
    weights = weights / jnp.sum(weights, axis=-1, keepdims=True)
    rounded = weights.astype(BF16)
    attended[0] = dot(rounded, v, 1, 0).astype(BF16)
    weight_grad = dot(out_grad, v, 1, 1).astype(BF16).astype(F32)
    mean = jnp.sum(weights * weight_grad, axis=-1, keepdims=True)
    score_grad = weights * (weight_grad - mean) * HD**-0.5
    upper = score_grad.astype(BF16)
    lower = (score_grad - upper.astype(F32)).astype(BF16)
    query_grad[0] = (dot(upper, k, 1, 0) + dot(lower, k, 1, 0)).astype(BF16)
    key_grad[...] += dot(upper, q, 0, 0) + dot(lower, q, 0, 0)
    value_grad[...] += dot(rounded, out_grad, 0, 0)

    @pl.when(head == GROUP - 1)
    def _():
        joined[:, :HD] = key_grad[...].astype(BF16)
        joined[:, HD:] = value_grad[...].astype(BF16)


def slab_kernel(x_inner, where, normed, *refs):
    joined, mine, theirs = refs[:4], refs[4:8], refs[8:12]
    heads = refs[12]
    x, y, core, high = where[0], where[1], where[2], where[3]
    for k in range(4):
        heads[lax.rem(high + k, 4)] = joined[k][...]
    for dy in range(4):
        row = lax.rem(y + dy, 4) * 2
        for half, outs in ((core, mine), (1 - core, theirs)):
            part = normed[row + half]
            for dx in range(4):
                term = dot(part, heads[lax.rem(x + dx, 4)], 0, 0).astype(BF16)
                if x_inner:
                    outs[dy][dx] = term
                else:
                    outs[dx][dy] = term


def spread_kernel(x_inner, where, hidden, inverse, *refs):
    joined, mine, theirs = refs[:4], refs[4:8], refs[8:12]
    spread, sums, heads, scaled = refs[12:16]
    x, y, core, high = where[0], where[1], where[2], where[3]
    for k in range(4):
        heads[lax.rem(high + k, 4)] = joined[k][...]
    for chunk in range(8):
        scaled[chunk] = hidden[0, :, chunk * BLOCK : (chunk + 1) * BLOCK].astype(F32) * inverse[0]
    products = jnp.zeros((SEQ, 1), F32)
    for dy in range(4):
        row = lax.rem(y + dy, 4) * 2
        for half, blocks in ((core, mine), (1 - core, theirs)):
            total = jnp.zeros((SEQ, BLOCK), F32)
            for dx in range(4):
                term = dot(heads[lax.rem(x + dx, 4)], piece(blocks, x_inner, dx, dy), 1, 1)
                total += term.astype(BF16).astype(F32)
            spread[row + half] = total
            products += jnp.sum(total * scaled[row + half], axis=-1, keepdims=True)
    sums[...] = products


def finish_kernel(has_old, spread, products, hidden, inverse, *refs):
    out = refs[1] if has_old else refs[0]
    for chunk in range(8):
        columns = slice(chunk * BLOCK, (chunk + 1) * BLOCK)
        scaled = hidden[0, :, columns].astype(F32) * inverse[0]
        out[0, :, columns] = (inverse[0] * (spread[chunk] - scaled * products[...])).astype(BF16)


def params():
    return pltpu.CompilerParams(vmem_limit_bytes=VMEM_BYTES)


def whole(shape):
    return pl.BlockSpec(shape, lambda *_: (0,) * len(shape))


def layer_of(depth, shape):
    return pl.BlockSpec((1,) + shape, lambda *_: (depth, 0, 0))


SCALARS = pl.BlockSpec(memory_space=pltpu.SMEM)
TILE = (SEQ, BLOCK)
ROW = (4, BLOCK, BLOCK)
CHUNKS = (8, SEQ, BLOCK)


def project(depth, x_inner, where, hidden, inverse, mine, theirs):
    return pl.pallas_call(
        functools.partial(project_kernel, x_inner),
        grid=(1,),
        out_shape=[jax.ShapeDtypeStruct(CHUNKS, BF16)] + [jax.ShapeDtypeStruct(TILE, F32)] * 4,
        in_specs=[SCALARS, layer_of(depth, (SEQ, 2048)), layer_of(depth, (SEQ, 1))] + [whole(ROW)] * 8,
        out_specs=[whole(CHUNKS)] + [whole(TILE)] * 4,
        scratch_shapes=[pltpu.VMEM((4,) + TILE, F32)],
        compiler_params=params(),
        cost_estimate=pl.CostEstimate(flops=2 * SEQ * 2048 * 1024, bytes_accessed=7 << 20, transcendentals=0),
    )(where, hidden, inverse, *mine, *theirs)


def attend(depth, parts, queries, cotangent, old):
    head = pl.BlockSpec((1, SEQ, HD), lambda g: (depth, 0, g))
    out = jax.ShapeDtypeStruct(queries.shape, BF16)
    return pl.pallas_call(
        functools.partial(attend_kernel, bool(old)),
        grid=(GROUP,),
        out_shape=[out, out, jax.ShapeDtypeStruct(TILE, BF16)],
        in_specs=[whole(TILE)] * 4 + [head] * 2 + [pl.BlockSpec(memory_space=pl.ANY)] * len(old),
        out_specs=[head, head, whole(TILE)],
        scratch_shapes=[pltpu.VMEM((SEQ, HD), BF16)] * 2 + [pltpu.VMEM((SEQ, HD), F32)] * 2,
        input_output_aliases={6: 0, 7: 1} if old else {},
        compiler_params=params(),
        cost_estimate=pl.CostEstimate(flops=64 * 2 * SEQ * SEQ * HD, bytes_accessed=4 << 20, transcendentals=GROUP * SEQ * SEQ),
    )(*parts, queries, cotangent, *old)


def slab_terms(x_inner, where, normed, joined):
    return pl.pallas_call(
        functools.partial(slab_kernel, x_inner),
        grid=(1,),
        out_shape=[jax.ShapeDtypeStruct(ROW, BF16)] * 8,
        in_specs=[SCALARS, whole(CHUNKS)] + [whole(TILE)] * 4,
        out_specs=[whole(ROW)] * 8,
        scratch_shapes=[pltpu.VMEM((4,) + TILE, BF16)],
        compiler_params=params(),
        cost_estimate=pl.CostEstimate(flops=2 * SEQ * 2048 * 1024, bytes_accessed=6 << 20, transcendentals=0),
    )(where, normed, *joined)


def spread_terms(depth, x_inner, where, hidden, inverse, joined, mine, theirs):
    return pl.pallas_call(
        functools.partial(spread_kernel, x_inner),
        grid=(1,),
        out_shape=[jax.ShapeDtypeStruct(CHUNKS, F32), jax.ShapeDtypeStruct((SEQ, 1), F32)],
        in_specs=[SCALARS, layer_of(depth, (SEQ, 2048)), layer_of(depth, (SEQ, 1))]
        + [whole(TILE)] * 4
        + [whole(ROW)] * 8,
        out_specs=[whole(CHUNKS), whole((SEQ, 1))],
        scratch_shapes=[pltpu.VMEM((4,) + TILE, BF16), pltpu.VMEM(CHUNKS, F32)],
        compiler_params=params(),
        cost_estimate=pl.CostEstimate(flops=2 * SEQ * 2048 * 1024, bytes_accessed=8 << 20, transcendentals=0),
    )(where, hidden, inverse, *joined, *mine, *theirs)


def finish(depth, spread, products, hidden, inverse, old):
    return pl.pallas_call(
        functools.partial(finish_kernel, bool(old)),
        grid=(1,),
        out_shape=jax.ShapeDtypeStruct(hidden.shape, BF16),
        in_specs=[whole(CHUNKS), whole((SEQ, 1)), layer_of(depth, (SEQ, 2048)), layer_of(depth, (SEQ, 1))]
        + [pl.BlockSpec(memory_space=pl.ANY)] * len(old),
        out_specs=layer_of(depth, (SEQ, 2048)),
        input_output_aliases={4: 0} if old else {},
        compiler_params=params(),
        cost_estimate=pl.CostEstimate(flops=4 * SEQ * 2048, bytes_accessed=4 << 20, transcendentals=0),
    )(spread, products, hidden, inverse, *old)


def shards(hidden, queries, cotangent, slabs):
    layer, core, high = lax.axis_index("layer"), lax.axis_index("dp") % 2, lax.axis_index("tensor")
    where = jnp.stack([layer // 4, layer % 4, core, high]).astype(jnp.int32)
    orders = (("x", "y"), ("y", "x"))

    half = lax.dynamic_slice_in_dim(slabs, core * BLOCK, BLOCK, 1)
    blocks = [shift(half[depth], SWAP) for depth in range(2)]
    floats = hidden.astype(F32)
    squares = jnp.sum(floats * floats, axis=-1)
    squares = squares + sum(shift(squares, along("z", k)) for k in (1, 2, 3))
    inverse = lax.rsqrt(squares / D + EPSILON)[..., None]

    mine, theirs, normed, parts = [], [], [], []
    for depth, (first, second) in enumerate(orders):
        mine.append(gather(blocks[depth], first, second))
        theirs.append([shift(row, CORE) for row in mine[depth]])
        made, *sums = project(depth, depth == 0, where, hidden, inverse, mine[depth], theirs[depth])
        normed.append(made)
        parts.append([sums[0]] + [shift(sums[k], along("z", k)) for k in (1, 2, 3)])

    old, old_hidden, slab_grads = [], [], []
    for depth, (first, second) in enumerate(orders):
        x_inner = depth == 0
        attended, query_grads, joined = attend(depth, parts[depth], queries, cotangent, old)
        old = [attended, query_grads]
        heads = [joined] + [shift(joined, along("z", -k)) for k in (1, 2, 3)]

        rows = slab_terms(x_inner, where, normed[depth], heads)
        sent = [shift(row, CORE) for row in rows[4:]]
        rows = [a.astype(F32) + b.astype(F32) for a, b in zip(rows[:4], sent)]
        total = scatter(rows, second, first)
        total = total + shift(total, LOW)
        total = shift(total, SWAP)
        other = shift(total, CORE)
        pair = jnp.where(core == 0, jnp.concatenate([total, other]), jnp.concatenate([other, total]))
        slab_grads.append(pair)

        spread, sums = spread_terms(depth, x_inner, where, hidden, inverse, heads, mine[depth], theirs[depth])
        flat = sums[:, 0]
        flat = (flat + sum(shift(flat, along("z", k)) for k in (1, 2, 3))) / D
        old_hidden = [finish(depth, spread, flat[:, None], hidden, inverse, old_hidden)]
    return old[0], old[1], old_hidden[0], jnp.stack(slab_grads)


def solution(mesh):
    tokens = P(None, ("layer", "dp"), "tensor")
    rows = P(None, "layer", "tensor")
    return jax.shard_map(
        shards,
        mesh=mesh,
        in_specs=(tokens, tokens, tokens, rows),
        out_specs=(tokens, tokens, tokens, rows),
        check_vma=False,
    )
```

```python
import functools

import jax
import jax.numpy as jnp
from jax import lax
from jax.experimental import pallas as pl
from jax.experimental.pallas import tpu as pltpu
from jax.sharding import PartitionSpec as P

D = 8192
HD = 128
GROUP = 8
SEQ = 256
EPSILON = 1e-05
BF16 = jnp.bfloat16
F32 = jnp.float32
AXES = ("layer", "dp", "tensor")
BLOCK = 256
VMEM_BYTES = 16 * 1024 * 1024
EXTRA = 16
LOG2E = 1.4426950408889634


def route(move):
    def flat(x, y, low, core, high):
        return ((x * 4 + y) * 4 + low * 2 + core) * 4 + high

    pairs = []
    for x in range(4):
        for y in range(4):
            for low in range(2):
                for core in range(2):
                    for high in range(4):
                        pairs.append((flat(x, y, low, core, high), flat(*move(x, y, low, core, high))))
    return pairs


def along_high(step):
    return route(lambda x, y, low, core, high: (x, y, low, core, (high + step) % 4))


CORE = route(lambda x, y, low, core, high: (x, y, low, 1 - core, high))
LOW = route(lambda x, y, low, core, high: (x, y, 1 - low, core, high))
BOTH = route(lambda x, y, low, core, high: (x, y, 1 - low, 1 - core, high))
SWAP = route(lambda x, y, low, core, high: (high, y, low, core, x))
STEPS = (1, 3, 2)


def shift(value, pairs):
    return lax.ppermute(value, AXES, pairs)


def after(value, *others):
    return lax.optimization_barrier((value, others))[0]


def dot(a, b, ca, cb):
    return lax.dot_general(a, b, (((ca,), (cb,)), ((), ())), preferred_element_type=F32)


def split_kernel(where, hidden, keep, send):
    core = where[2]
    for mine in range(2):

        @pl.when(core == mine)
        def _():
            for j in range(4):
                for out, half in ((keep, mine), (send, 1 - mine)):
                    first = (2 * j + half) * BLOCK
                    out[0, j] = hidden[0, :, first : first + BLOCK]


def norm_kernel(keep, sib, inverse, sib_inverse, normed, turned):
    for s, states, scale in ((0, keep, inverse), (1, sib, sib_inverse)):
        for j in range(4):
            part = (states[0, j].astype(F32) * scale[0]).astype(BF16)
            normed[0, s, j] = part
            turned[0, s, j] = part.T


def project_kernel(where, normed, blocks, out):
    out[0] = sum(dot(normed[0, 0, j], blocks[0, j], 1, 0) for j in range(4))


def merge_kernel(own, got, *outs):
    for k in range(4):
        outs[k][...] = own[k] + got[k]


def attend_kernel(has_old, *refs):
    parts, refs = refs[:4], refs[4:]
    query, cotangent = refs[:2]
    refs = refs[4:] if has_old else refs[2:]
    attended, query_grad, joined = refs
    projected = (parts[0][...] + parts[1][...]) + (parts[2][...] + parts[3][...])
    rounded = projected.astype(BF16)
    k, v = rounded[:, :HD], rounded[:, HD:]
    kt, vt = k.T, v.T
    to = lax.broadcasted_iota(jnp.int32, (SEQ, SEQ), 0)
    at = lax.broadcasted_iota(jnp.int32, (SEQ, SEQ), 1)
    key_grad = jnp.zeros((SEQ, HD), F32)
    value_grad = jnp.zeros((SEQ, HD), F32)
    for head in range(GROUP):
        columns = slice(head * HD, (head + 1) * HD)
        q, out_grad = query[0, :, columns], cotangent[0, :, columns]
        scores = jnp.where(at >= to, dot(k, q, 1, 1), -1e30)
        weights = jnp.exp2((scores - jnp.max(scores, axis=0, keepdims=True)) * (HD**-0.5 * LOG2E))
        weights = weights * (1.0 / jnp.sum(weights, axis=0, keepdims=True))
        held = weights.astype(BF16)
        attended[0, :, columns] = dot(vt, held, 1, 0).T.astype(BF16)
        weight_grad = dot(v, out_grad, 1, 1).astype(BF16).astype(F32)
        mean = jnp.sum(weights * weight_grad, axis=0, keepdims=True)
        score_grad = weights * (weight_grad - mean)
        upper = score_grad.astype(BF16)
        lower = (score_grad - upper.astype(F32)).astype(BF16)
        grad = dot(kt, upper, 1, 0) + dot(kt, lower, 1, 0)
        query_grad[0, :, columns] = (grad * HD**-0.5).T.astype(BF16)
        key_grad += dot(upper, q, 1, 0) + dot(lower, q, 1, 0)
        value_grad += dot(held, out_grad, 1, 0)
    grads = jnp.concatenate([key_grad * HD**-0.5, value_grad], axis=1).astype(BF16)
    joined[:SEQ] = grads
    shares = jnp.sum(grads.astype(F32) * projected, axis=1, keepdims=True)
    row = jnp.broadcast_to(shares, (SEQ, 128)).T[:EXTRA]
    at_row = lax.broadcasted_iota(jnp.int32, (EXTRA, SEQ), 0)
    terms = jnp.zeros((EXTRA, SEQ), F32)
    for index, term in enumerate(three(row)):
        terms = jnp.where(at_row == index, term.astype(F32), terms)
    joined[SEQ:] = terms.astype(BF16)


def three(value):
    terms = []
    for _ in range(3):
        terms.append(value.astype(BF16))
        value = value - terms[-1].astype(F32)
    return terms


def slab_kernel(where, turned, own, sib, out):
    k = lax.rem(pl.program_id(0) - where[3] + 4, 4)
    for j in range(4):
        term = dot(turned[0, 0, j], own[k, :SEQ], 1, 0).astype(BF16).astype(F32)
        term += dot(turned[0, 1, j], sib[k, :SEQ], 1, 0).astype(BF16).astype(F32)
        out[j] = term.astype(BF16)


def total_kernel(where, parts, moved, kept):
    total = parts[0].astype(F32)
    for k in range(1, 16):
        total += parts[k].astype(F32)

    @pl.when(pl.program_id(0) == 0)
    def _():
        moved[...] = total

    @pl.when(pl.program_id(0) == 1)
    def _():
        kept[...] = total


def spread_kernel(where, keep, sib, inverse, sib_inverse, own_heads, sib_heads, blocks, own_out, sib_out, products):
    @pl.when(pl.program_id(0) == 0)
    def _():
        for s, heads in enumerate((own_heads, sib_heads)):
            rows = [dot(heads[k, SEQ:], jnp.ones((EXTRA, BLOCK), BF16), 0, 0) for k in range(4)]
            products[s] = sum(rows) / D

    for s, heads, states, scale, out in (
        (1, sib_heads, sib, sib_inverse, sib_out),
        (0, own_heads, keep, inverse, own_out),
    ):
        spread = jnp.zeros((SEQ, BLOCK), F32)
        for b in range(4):
            term = dot(heads[lax.rem(b - where[3] + 4, 4), :SEQ], blocks[b, 0], 1, 1)
            spread += term.astype(BF16).astype(F32)
        scaled = states[0, 0].astype(F32) * scale[0]
        out[0] = (scale[0] * (spread - scaled * products[s])).astype(BF16)


def unsplit_kernel(has_old, where, keep, got, *refs):
    out = refs[-1]
    core = where[2]
    for mine in range(2):

        @pl.when(core == mine)
        def _():
            for j in range(4):
                for part, half in ((keep, mine), (got, 1 - mine)):
                    first = (2 * j + half) * BLOCK
                    out[0, :, first : first + BLOCK] = part[j]


def place_kernel(where, *refs):
    out = refs[8]
    core, low = where[2], where[4]
    for depth in range(2):
        for k in range(4):
            half = core if k % 2 == 0 else 1 - core
            quarter = low if k < 2 else 1 - low
            first = pl.multiple_of(half * 256 + quarter * 128, 128)
            out[depth, pl.ds(first, 128), :] = refs[4 * depth + k][...].astype(F32)


TILE = (SEQ, BLOCK)
ANY = pl.BlockSpec(memory_space=pl.ANY)


def shape(dims, dtype):
    return jax.ShapeDtypeStruct(dims, dtype)


def whole(*dims):
    return pl.BlockSpec(dims, lambda *_: (0,) * len(dims))


def layer_of(depth, *dims):
    return pl.BlockSpec((1,) + dims, lambda *_: (depth,) + (0,) * len(dims))


def run(kernel, grid, outs, in_specs, out_specs, args, scratch=(), aliases={}, megaflops=1, scalars=True):
    return pl.pallas_call(
        kernel,
        out_shape=outs,
        grid_spec=pltpu.PrefetchScalarGridSpec(
            num_scalar_prefetch=1 if scalars else 0,
            grid=(grid,),
            in_specs=in_specs,
            out_specs=out_specs,
            scratch_shapes=scratch,
        ),
        input_output_aliases=aliases,
        compiler_params=pltpu.CompilerParams(vmem_limit_bytes=VMEM_BYTES),
        cost_estimate=pl.CostEstimate(flops=megaflops * 10**6, bytes_accessed=6 << 20, transcendentals=0),
    )(*args)


def split(where, hidden):
    parts = pl.BlockSpec((1, 4) + TILE, lambda d, w: (d, 0, 0, 0))
    return run(
        split_kernel,
        2,
        [shape((2, 4) + TILE, BF16)] * 2,
        [pl.BlockSpec((1, SEQ, 2048), lambda d, w: (d, 0, 0))],
        [parts, parts],
        (where, hidden),
    )


def normalize(states):
    pair = pl.BlockSpec((1, 4) + TILE, lambda d: (d, 0, 0, 0))
    scale = pl.BlockSpec((1, SEQ, 1), lambda d: (d, 0, 0))
    out = pl.BlockSpec((1, 2, 4) + TILE, lambda d: (d, 0, 0, 0, 0))
    return run(
        norm_kernel,
        2,
        [shape((2, 2, 4) + TILE, BF16)] * 2,
        [pair, pair, scale, scale],
        [out, out],
        states,
        scalars=False,
    )


def project(depth, side, where, normed, blocks):
    return run(
        project_kernel,
        4,
        shape((4,) + TILE, F32),
        [
            pl.BlockSpec((1, 1, 4) + TILE, lambda k, w: (depth, side, 0, 0, 0)),
            pl.BlockSpec((1, 4) + TILE, lambda k, w: (lax.rem(k + w[3], 4), 0, 0, 0)),
        ],
        pl.BlockSpec((1,) + TILE, lambda k, w: (k, 0, 0)),
        (where, normed, blocks),
        megaflops=537,
    )


def merge(own, got):
    return run(
        merge_kernel,
        1,
        [shape(TILE, F32)] * 4,
        [whole(4, *TILE)] * 2,
        [whole(*TILE)] * 4,
        (own, got),
        scalars=False,
    )


def attend(depth, parts, queries, cotangent, old):
    heads = layer_of(depth, SEQ, GROUP * HD)
    return run(
        functools.partial(attend_kernel, bool(old)),
        1,
        [shape(queries.shape, BF16)] * 2 + [shape((SEQ + EXTRA, BLOCK), BF16)],
        [whole(*TILE)] * 4 + [heads] * 2 + [ANY] * len(old),
        [heads, heads, whole(SEQ + EXTRA, BLOCK)],
        (*parts, queries, cotangent, *old),
        aliases={6: 0, 7: 1} if old else {},
        megaflops=5000,
        scalars=False,
    )


def slab_terms(depth, where, turned, own, sib):
    return run(
        slab_kernel,
        4,
        shape((16,) + TILE, BF16),
        [layer_of(depth, 2, 4, *TILE)] + [whole(4, SEQ + EXTRA, BLOCK)] * 2,
        pl.BlockSpec((4,) + TILE, lambda b, w: (b, 0, 0)),
        (where, turned, own, sib),
        megaflops=1074,
    )


def plane_total(where, parts):
    quarter = pl.BlockSpec((16, 128, BLOCK), lambda s, w: (0, lax.rem(w[4] + 1 + s, 2), 0))
    return run(
        total_kernel,
        2,
        [shape((128, BLOCK), F32)] * 2,
        [quarter],
        [whole(128, BLOCK)] * 2,
        (where, parts),
    )


def spread_out(depth, where, states, own, sib, blocks):
    state = pl.BlockSpec((1, 1) + TILE, lambda j, w: (depth, j, 0, 0))
    row = pl.BlockSpec((4, 1) + TILE, lambda j, w: (0, j, 0, 0))
    out = pl.BlockSpec((1,) + TILE, lambda j, w: (j, 0, 0))
    return run(
        spread_kernel,
        4,
        [shape((4,) + TILE, BF16)] * 2,
        [state] * 2 + [layer_of(depth, SEQ, 1)] * 2 + [whole(4, SEQ + EXTRA, BLOCK)] * 2 + [row],
        [out, out],
        (where, *states, own, sib, blocks),
        [pltpu.VMEM((2,) + TILE, F32)],
        megaflops=1074,
    )


def unsplit(depth, where, keep, got, dims, old):
    return run(
        functools.partial(unsplit_kernel, bool(old)),
        1,
        shape(dims, BF16),
        [whole(4, *TILE)] * 2 + [ANY] * len(old),
        layer_of(depth, SEQ, 2048),
        (where, keep, got, *old),
        aliases={3: 0} if old else {},
    )


def place(where, quarters):
    return run(
        place_kernel,
        1,
        shape((2, 512, BLOCK), F32),
        [whole(128, BLOCK)] * 8,
        whole(2, 512, BLOCK),
        (where, *quarters),
    )


def shards(hidden, queries, cotangent, slabs):
    layer, dp, high = lax.axis_index("layer"), lax.axis_index("dp"), lax.axis_index("tensor")
    core, low = dp % 2, dp // 2
    where = jnp.stack([layer // 4, layer % 4, core, high, low]).astype(jnp.int32)

    half = lax.dynamic_slice_in_dim(slabs, core * BLOCK, BLOCK, 1)
    owned = shift(half[0], SWAP)
    keep, send = split(where, hidden)
    sib = shift(send, CORE)
    floats = hidden.astype(F32)
    squares = jnp.sum(floats * floats, axis=-1)
    owned = after(owned, send, squares)
    squares = squares + sum(shift(squares, along_high(k)) for k in (1, 2, 3))
    inverse = lax.rsqrt(squares / D + EPSILON)
    states = (keep, sib, inverse[..., None], shift(inverse, CORE)[..., None])
    normed, turned = normalize(states)

    blocks, sums = [], []
    for depth in range(2):
        sent = jnp.broadcast_to(owned, (16,) + TILE)
        if depth == 1:
            sent = after(sent, *sums[0])
        got = lax.all_to_all(sent, "layer", 0, 0, tiled=True)
        if depth == 0:
            owned = shift(after(half[1], sent), SWAP)
            got = after(got, owned)
        blocks.append(got.reshape((4, 4) + TILE))
        got = shift(project(depth, 1, where, normed, blocks[depth]), CORE)
        sums.append(merge(project(depth, 0, where, normed, blocks[depth]), got))

    old, hidden_grads, quarters = [], [], []
    for depth in range(2):
        arrived = {k: shift(sums[depth][k], along_high(k)) for k in STEPS}
        parts = [sums[depth][0]] + [arrived[k] for k in (1, 2, 3)]
        if depth == 1:
            parts = list(after(tuple(parts), own_out))
        attended, query_grads, joined = attend(depth, parts, queries, cotangent, old)
        old = [attended, query_grads]
        arrived = {k: shift(joined, along_high(-k)) for k in STEPS}
        own = jnp.stack([joined] + [arrived[k] for k in (1, 2, 3)])
        sib_heads = shift(own, CORE)
        if depth == 0:
            sums[1] = after(tuple(sums[1]), own)
        terms = slab_terms(depth, where, turned, own, sib_heads)
        own = after(own, terms)
        terms = lax.all_to_all(terms, "layer", 0, 0, tiled=True)
        own_out, sib_out = spread_out(depth, where, states, own, sib_heads, blocks[depth])
        got = shift(sib_out, CORE)
        hidden_grads = [unsplit(depth, where, own_out, got, hidden.shape, hidden_grads)]
        if depth == 1:
            terms = after(terms, own_out, *quarters)
        moved, kept = plane_total(where, terms)
        total = shift((kept + shift(moved, LOW)).astype(BF16), SWAP)
        quarters += [total] + [shift(total, pairs) for pairs in (CORE, LOW, BOTH)]
    return old[0], old[1], hidden_grads[0], place(where, quarters)


def solution(mesh):
    tokens = P(None, ("layer", "dp"), "tensor")
    rows = P(None, "layer", "tensor")
    return jax.shard_map(
        shards,
        mesh=mesh,
        in_specs=(tokens, tokens, tokens, rows),
        out_specs=(tokens, tokens, tokens, rows),
        check_vma=False,
    )
```

```python
import functools

import jax
import jax.numpy as jnp
from jax import lax
from jax.experimental import pallas as pl
from jax.experimental.pallas import tpu as pltpu
from jax.sharding import PartitionSpec as P

D = 8192
HD = 128
GROUP = 8
SEQ = 256
EPSILON = 1e-05
BF16 = jnp.bfloat16
F32 = jnp.float32
AXES = ("layer", "dp", "tensor")
BLOCK = 256
VMEM_BYTES = 16 * 1024 * 1024
EXTRA = 16
LOG2E = 1.4426950408889634


def route(move):
    def flat(x, y, low, core, high):
        return ((x * 4 + y) * 4 + low * 2 + core) * 4 + high

    pairs = []
    for x in range(4):
        for y in range(4):
            for low in range(2):
                for core in range(2):
                    for high in range(4):
                        pairs.append((flat(x, y, low, core, high), flat(*move(x, y, low, core, high))))
    return pairs


def along_high(step):
    return route(lambda x, y, low, core, high: (x, y, low, core, (high + step) % 4))


CORE = route(lambda x, y, low, core, high: (x, y, low, 1 - core, high))
LOW = route(lambda x, y, low, core, high: (x, y, 1 - low, core, high))
BOTH = route(lambda x, y, low, core, high: (x, y, 1 - low, 1 - core, high))
SWAP = route(lambda x, y, low, core, high: (high, y, low, core, x))
STEPS = (1, 3, 2)


def shift(value, pairs):
    return lax.ppermute(value, AXES, pairs)


def after(value, *others):
    return lax.optimization_barrier((value, others))[0]


def dot(a, b, ca, cb):
    return lax.dot_general(a, b, (((ca,), (cb,)), ((), ())), preferred_element_type=F32)


def split_kernel(where, hidden, keep, send):
    core = where[2]
    for mine in range(2):

        @pl.when(core == mine)
        def _():
            for j in range(4):
                for out, half in ((keep, mine), (send, 1 - mine)):
                    first = (2 * j + half) * BLOCK
                    out[0, j] = hidden[0, :, first : first + BLOCK]


def norm_kernel(keep, sib, inverse, sib_inverse, normed, turned):
    for s, states, scale in ((0, keep, inverse), (1, sib, sib_inverse)):
        for j in range(4):
            part = (states[0, j].astype(F32) * scale[0]).astype(BF16)
            normed[0, s, j] = part
            turned[0, s, j] = part.T


def project_kernel(where, normed, blocks, out):
    out[0] = sum(dot(normed[0, 0, j], blocks[0, j], 1, 0) for j in range(4))


def merge_kernel(own, got, *outs):
    for k in range(4):
        outs[k][...] = own[k] + got[k]


def attend_kernel(has_old, *refs):
    parts, refs = refs[:4], refs[4:]
    query, cotangent = refs[:2]
    refs = refs[4:] if has_old else refs[2:]
    attended, query_grad, joined = refs
    projected = (parts[0][...] + parts[1][...]) + (parts[2][...] + parts[3][...])
    rounded = projected.astype(BF16)
    k, v = rounded[:, :HD], rounded[:, HD:]
    kt, vt = k.T, v.T
    to = lax.broadcasted_iota(jnp.int32, (SEQ, SEQ), 0)
    at = lax.broadcasted_iota(jnp.int32, (SEQ, SEQ), 1)
    key_grad = jnp.zeros((SEQ, HD), F32)
    value_grad = jnp.zeros((SEQ, HD), F32)
    for head in range(GROUP):
        columns = slice(head * HD, (head + 1) * HD)
        q, out_grad = query[0, :, columns], cotangent[0, :, columns]
        scores = jnp.where(at >= to, dot(k, q, 1, 1), -1e30)
        weights = jnp.exp2((scores - jnp.max(scores, axis=0, keepdims=True)) * (HD**-0.5 * LOG2E))
        weights = weights * (1.0 / jnp.sum(weights, axis=0, keepdims=True))
        held = weights.astype(BF16)
        attended[0, :, columns] = dot(vt, held, 1, 0).T.astype(BF16)
        weight_grad = dot(v, out_grad, 1, 1).astype(BF16).astype(F32)
        mean = jnp.sum(weights * weight_grad, axis=0, keepdims=True)
        score_grad = weights * (weight_grad - mean)
        upper = score_grad.astype(BF16)
        lower = (score_grad - upper.astype(F32)).astype(BF16)
        grad = dot(kt, upper, 1, 0) + dot(kt, lower, 1, 0)
        query_grad[0, :, columns] = (grad * HD**-0.5).T.astype(BF16)
        key_grad += dot(upper, q, 1, 0) + dot(lower, q, 1, 0)
        value_grad += dot(held, out_grad, 1, 0)
    grads = jnp.concatenate([key_grad * HD**-0.5, value_grad], axis=1).astype(BF16)
    joined[:SEQ] = grads
    shares = jnp.sum(grads.astype(F32) * projected, axis=1, keepdims=True)
    row = jnp.broadcast_to(shares, (SEQ, 128)).T[:EXTRA]
    at_row = lax.broadcasted_iota(jnp.int32, (EXTRA, SEQ), 0)
    terms = jnp.zeros((EXTRA, SEQ), F32)
    for index, term in enumerate(three(row)):
        terms = jnp.where(at_row == index, term.astype(F32), terms)
    joined[SEQ:] = terms.astype(BF16)


def three(value):
    terms = []
    for _ in range(3):
        terms.append(value.astype(BF16))
        value = value - terms[-1].astype(F32)
    return terms


def slab_kernel(where, turned, own, sib, out):
    k = lax.rem(pl.program_id(0) - where[3] + 4, 4)
    for j in range(4):
        term = dot(turned[0, 0, j], own[k, :SEQ], 1, 0).astype(BF16).astype(F32)
        term += dot(turned[0, 1, j], sib[k, :SEQ], 1, 0).astype(BF16).astype(F32)
        out[j] = term.astype(BF16)


def total_kernel(parts, out):
    total = parts[0].astype(F32)
    for k in range(1, 16):
        total += parts[k].astype(F32)
    out[...] = total.astype(BF16)


def spread_kernel(where, keep, sib, inverse, sib_inverse, own_heads, sib_heads, blocks, own_out, sib_out, products):
    @pl.when(pl.program_id(0) == 0)
    def _():
        for s, heads in enumerate((own_heads, sib_heads)):
            rows = [dot(heads[k, SEQ:], jnp.ones((EXTRA, BLOCK), BF16), 0, 0) for k in range(4)]
            products[s] = sum(rows) / D

    for s, heads, states, scale, out in (
        (1, sib_heads, sib, sib_inverse, sib_out),
        (0, own_heads, keep, inverse, own_out),
    ):
        spread = jnp.zeros((SEQ, BLOCK), F32)
        for b in range(4):
            term = dot(heads[lax.rem(b - where[3] + 4, 4), :SEQ], blocks[b, 0], 1, 1)
            spread += term.astype(BF16).astype(F32)
        scaled = states[0, 0].astype(F32) * scale[0]
        out[0] = (scale[0] * (spread - scaled * products[s])).astype(BF16)


def unsplit_kernel(has_old, where, keep, got, *refs):
    out = refs[-1]
    core = where[2]
    for mine in range(2):

        @pl.when(core == mine)
        def _():
            for j in range(4):
                for part, half in ((keep, mine), (got, 1 - mine)):
                    first = (2 * j + half) * BLOCK
                    out[0, :, first : first + BLOCK] = part[j]


def place_kernel(where, *refs):
    out = refs[8]
    for depth in range(2):
        for k in range(2):
            first = pl.multiple_of((where[2] if k == 0 else 1 - where[2]) * BLOCK, BLOCK)
            near, far = refs[4 * depth + k], refs[4 * depth + 2 + k]
            out[depth, pl.ds(first, BLOCK), :] = near[...].astype(F32) + far[...].astype(F32)


TILE = (SEQ, BLOCK)
ANY = pl.BlockSpec(memory_space=pl.ANY)


def shape(dims, dtype):
    return jax.ShapeDtypeStruct(dims, dtype)


def whole(*dims):
    return pl.BlockSpec(dims, lambda *_: (0,) * len(dims))


def layer_of(depth, *dims):
    return pl.BlockSpec((1,) + dims, lambda *_: (depth,) + (0,) * len(dims))


def run(kernel, grid, outs, in_specs, out_specs, args, scratch=(), aliases={}, megaflops=1, scalars=True):
    return pl.pallas_call(
        kernel,
        out_shape=outs,
        grid_spec=pltpu.PrefetchScalarGridSpec(
            num_scalar_prefetch=1 if scalars else 0,
            grid=(grid,),
            in_specs=in_specs,
            out_specs=out_specs,
            scratch_shapes=scratch,
        ),
        input_output_aliases=aliases,
        compiler_params=pltpu.CompilerParams(vmem_limit_bytes=VMEM_BYTES),
        cost_estimate=pl.CostEstimate(flops=megaflops * 10**6, bytes_accessed=6 << 20, transcendentals=0),
    )(*args)


def split(where, hidden):
    parts = pl.BlockSpec((1, 4) + TILE, lambda d, w: (d, 0, 0, 0))
    return run(
        split_kernel,
        2,
        [shape((2, 4) + TILE, BF16)] * 2,
        [pl.BlockSpec((1, SEQ, 2048), lambda d, w: (d, 0, 0))],
        [parts, parts],
        (where, hidden),
    )


def normalize(states):
    pair = pl.BlockSpec((1, 4) + TILE, lambda d: (d, 0, 0, 0))
    scale = pl.BlockSpec((1, SEQ, 1), lambda d: (d, 0, 0))
    out = pl.BlockSpec((1, 2, 4) + TILE, lambda d: (d, 0, 0, 0, 0))
    return run(
        norm_kernel,
        2,
        [shape((2, 2, 4) + TILE, BF16)] * 2,
        [pair, pair, scale, scale],
        [out, out],
        states,
        scalars=False,
    )


def project(depth, side, where, normed, blocks):
    return run(
        project_kernel,
        4,
        shape((4,) + TILE, F32),
        [
            pl.BlockSpec((1, 1, 4) + TILE, lambda k, w: (depth, side, 0, 0, 0)),
            pl.BlockSpec((1, 4) + TILE, lambda k, w: (lax.rem(k + w[3], 4), 0, 0, 0)),
        ],
        pl.BlockSpec((1,) + TILE, lambda k, w: (k, 0, 0)),
        (where, normed, blocks),
        megaflops=537,
    )


def merge(own, got):
    return run(
        merge_kernel,
        1,
        [shape(TILE, F32)] * 4,
        [whole(4, *TILE)] * 2,
        [whole(*TILE)] * 4,
        (own, got),
        scalars=False,
    )


def attend(depth, parts, queries, cotangent, old):
    heads = layer_of(depth, SEQ, GROUP * HD)
    return run(
        functools.partial(attend_kernel, bool(old)),
        1,
        [shape(queries.shape, BF16)] * 2 + [shape((SEQ + EXTRA, BLOCK), BF16)],
        [whole(*TILE)] * 4 + [heads] * 2 + [ANY] * len(old),
        [heads, heads, whole(SEQ + EXTRA, BLOCK)],
        (*parts, queries, cotangent, *old),
        aliases={6: 0, 7: 1} if old else {},
        megaflops=5000,
        scalars=False,
    )


def slab_terms(depth, where, turned, own, sib):
    return run(
        slab_kernel,
        4,
        shape((16,) + TILE, BF16),
        [layer_of(depth, 2, 4, *TILE)] + [whole(4, SEQ + EXTRA, BLOCK)] * 2,
        pl.BlockSpec((4,) + TILE, lambda b, w: (b, 0, 0)),
        (where, turned, own, sib),
        megaflops=1074,
    )


def plane_total(parts):
    return run(
        total_kernel,
        4,
        shape(TILE, BF16),
        [pl.BlockSpec((16, 64, BLOCK), lambda s: (0, s, 0))],
        pl.BlockSpec((64, BLOCK), lambda s: (s, 0)),
        (parts,),
        scalars=False,
    )


def spread_out(depth, where, states, own, sib, blocks):
    state = pl.BlockSpec((1, 1) + TILE, lambda j, w: (depth, j, 0, 0))
    row = pl.BlockSpec((4, 1) + TILE, lambda j, w: (0, j, 0, 0))
    out = pl.BlockSpec((1,) + TILE, lambda j, w: (j, 0, 0))
    return run(
        spread_kernel,
        4,
        [shape((4,) + TILE, BF16)] * 2,
        [state] * 2 + [layer_of(depth, SEQ, 1)] * 2 + [whole(4, SEQ + EXTRA, BLOCK)] * 2 + [row],
        [out, out],
        (where, *states, own, sib, blocks),
        [pltpu.VMEM((2,) + TILE, F32)],
        megaflops=1074,
    )


def unsplit(depth, where, keep, got, dims, old):
    return run(
        functools.partial(unsplit_kernel, bool(old)),
        1,
        shape(dims, BF16),
        [whole(4, *TILE)] * 2 + [ANY] * len(old),
        layer_of(depth, SEQ, 2048),
        (where, keep, got, *old),
        aliases={3: 0} if old else {},
    )


def place(where, quarters):
    return run(
        place_kernel,
        1,
        shape((2, 512, BLOCK), F32),
        [whole(*TILE)] * 8,
        whole(2, 512, BLOCK),
        (where, *quarters),
    )


def shards(hidden, queries, cotangent, slabs):
    layer, dp, high = lax.axis_index("layer"), lax.axis_index("dp"), lax.axis_index("tensor")
    core, low = dp % 2, dp // 2
    where = jnp.stack([layer // 4, layer % 4, core, high, low]).astype(jnp.int32)

    half = lax.dynamic_slice_in_dim(slabs, core * BLOCK, BLOCK, 1)
    owned = shift(half[0], SWAP)
    keep, send = split(where, hidden)
    sib = shift(send, CORE)
    floats = hidden.astype(F32)
    squares = jnp.sum(floats * floats, axis=-1)
    owned = after(owned, send, squares)
    squares = squares + sum(shift(squares, along_high(k)) for k in (1, 2, 3))
    inverse = lax.rsqrt(squares / D + EPSILON)
    states = (keep, sib, inverse[..., None], shift(inverse, CORE)[..., None])
    normed, turned = normalize(states)

    def fetch(sent):
        return lax.all_to_all(sent, "layer", 0, 0, tiled=True)

    def partial(depth, part):
        away = shift(project(depth, 1, where, normed, part), CORE)
        return merge(project(depth, 0, where, normed, part), away)

    def reduce_heads(sums):
        arrived = {k: shift(sums[k], along_high(k)) for k in STEPS}
        return [sums[0]] + [arrived[k] for k in (1, 2, 3)]

    def gather_heads(joined):
        arrived = {k: shift(joined, along_high(-k)) for k in STEPS}
        return jnp.stack([joined] + [arrived[k] for k in (1, 2, 3)])

    def spread(placed):
        return [placed] + [shift(placed, pairs) for pairs in (CORE, LOW, BOTH)]

    sent = jnp.broadcast_to(owned, (16,) + TILE)
    blocks = fetch(sent)
    owned = shift(after(half[1], sent), SWAP)
    sent = jnp.broadcast_to(owned, (16,) + TILE)
    blocks0 = after(blocks, owned).reshape((4, 4) + TILE)
    sums = partial(0, blocks0)
    sent = after(sent, *sums)
    parts = reduce_heads(sums)
    parts, blocks1 = lax.optimization_barrier((parts, fetch(sent)))
    blocks1 = blocks1.reshape((4, 4) + TILE)
    attended, query_grads, joined = attend(0, parts, queries, cotangent, [])
    sums = partial(1, blocks1)

    joined, parts = lax.optimization_barrier((joined, reduce_heads(sums)))
    own0 = gather_heads(joined)
    attended, query_grads, joined = attend(1, parts, queries, cotangent, [attended, query_grads])
    own0, joined = lax.optimization_barrier((own0, joined))
    sib0 = shift(own0, CORE)
    terms0 = slab_terms(0, where, turned, own0, sib0)
    own0, sib0 = after((own0, sib0), terms0)
    terms0 = fetch(terms0)

    own1 = gather_heads(joined)
    sib1 = shift(own1, CORE)
    terms1 = slab_terms(1, where, turned, own1, sib1)
    own1, sib1, own0 = after((own1, sib1, own0), terms1)
    terms1 = fetch(terms1)
    own_out, sib_out = spread_out(0, where, states, own0, sib0, blocks0)
    hidden_grads = unsplit(0, where, own_out, shift(sib_out, CORE), hidden.shape, [])
    own_out, sib_out = spread_out(1, where, states, own1, sib1, blocks1)
    hidden_grads = unsplit(1, where, own_out, shift(sib_out, CORE), hidden.shape, [hidden_grads])

    total = after(plane_total(terms0), own_out)
    quarters = spread(shift(total, SWAP))
    total = plane_total(after(terms1, total, hidden_grads))
    quarters += spread(shift(total, SWAP))
    return attended, query_grads, hidden_grads, place(where, quarters)


def solution(mesh):
    tokens = P(None, ("layer", "dp"), "tensor")
    rows = P(None, "layer", "tensor")
    return jax.shard_map(
        shards,
        mesh=mesh,
        in_specs=(tokens, tokens, tokens, rows),
        out_specs=(tokens, tokens, tokens, rows),
        check_vma=False,
    )
```

```python
import functools

import jax
import jax.numpy as jnp
from jax import lax
from jax.experimental import pallas as pl
from jax.experimental.pallas import tpu as pltpu
from jax.sharding import PartitionSpec as P

D = 8192
HD = 128
GROUP = 8
SEQ = 256
EPSILON = 1e-05
BF16 = jnp.bfloat16
F32 = jnp.float32
AXES = ("layer", "dp", "tensor")
BLOCK = 256
VMEM_BYTES = 16 * 1024 * 1024
EXTRA = 16
LOG2E = 1.4426950408889634


def route(move):
    def flat(x, y, low, core, high):
        return ((x * 4 + y) * 4 + low * 2 + core) * 4 + high

    pairs = []
    for x in range(4):
        for y in range(4):
            for low in range(2):
                for core in range(2):
                    for high in range(4):
                        pairs.append((flat(x, y, low, core, high), flat(*move(x, y, low, core, high))))
    return pairs


def along_high(step):
    return route(lambda x, y, low, core, high: (x, y, low, core, (high + step) % 4))


CORE = route(lambda x, y, low, core, high: (x, y, low, 1 - core, high))
LOW = route(lambda x, y, low, core, high: (x, y, 1 - low, core, high))
BOTH = route(lambda x, y, low, core, high: (x, y, 1 - low, 1 - core, high))
SWAP = route(lambda x, y, low, core, high: (high, y, low, core, x))
STEPS = (1, 3, 2)


def shift(value, pairs):
    return lax.ppermute(value, AXES, pairs)


def after(value, *others):
    return lax.optimization_barrier((value, others))[0]


def dot(a, b, ca, cb):
    return lax.dot_general(a, b, (((ca,), (cb,)), ((), ())), preferred_element_type=F32)


def split_kernel(where, hidden, keep, send):
    core = where[2]
    for mine in range(2):

        @pl.when(core == mine)
        def _():
            for j in range(4):
                for out, half in ((keep, mine), (send, 1 - mine)):
                    first = (2 * j + half) * BLOCK
                    out[0, j] = hidden[0, :, first : first + BLOCK]


def norm_kernel(keep, sib, inverse, sib_inverse, normed, turned):
    for s, states, scale in ((0, keep, inverse), (1, sib, sib_inverse)):
        for j in range(4):
            part = (states[0, j].astype(F32) * scale[0]).astype(BF16)
            normed[0, s, j] = part
            turned[0, s, j] = part.T


def project_kernel(where, normed, blocks, out):
    out[0] = sum(dot(normed[0, 0, j], blocks[0, j], 1, 0) for j in range(4))


def merge_kernel(own, got, *outs):
    for k in range(4):
        outs[k][...] = own[k] + got[k]


def attend_kernel(has_old, *refs):
    parts, refs = refs[:4], refs[4:]
    query, cotangent = refs[:2]
    refs = refs[4:] if has_old else refs[2:]
    attended, query_grad, joined = refs
    projected = (parts[0][...] + parts[1][...]) + (parts[2][...] + parts[3][...])
    rounded = projected.astype(BF16)
    k, v = rounded[:, :HD], rounded[:, HD:]
    kt, vt = k.T, v.T
    to = lax.broadcasted_iota(jnp.int32, (SEQ, SEQ), 0)
    at = lax.broadcasted_iota(jnp.int32, (SEQ, SEQ), 1)
    key_grad = jnp.zeros((SEQ, HD), F32)
    value_grad = jnp.zeros((SEQ, HD), F32)
    for head in range(GROUP):
        columns = slice(head * HD, (head + 1) * HD)
        q, out_grad = query[0, :, columns], cotangent[0, :, columns]
        scores = jnp.where(at >= to, dot(k, q, 1, 1), -1e30)
        weights = jnp.exp2((scores - jnp.max(scores, axis=0, keepdims=True)) * (HD**-0.5 * LOG2E))
        weights = weights * (1.0 / jnp.sum(weights, axis=0, keepdims=True))
        held = weights.astype(BF16)
        attended[0, :, columns] = dot(vt, held, 1, 0).T.astype(BF16)
        weight_grad = dot(v, out_grad, 1, 1).astype(BF16).astype(F32)
        mean = jnp.sum(weights * weight_grad, axis=0, keepdims=True)
        score_grad = weights * (weight_grad - mean)
        upper = score_grad.astype(BF16)
        lower = (score_grad - upper.astype(F32)).astype(BF16)
        grad = dot(kt, upper, 1, 0) + dot(kt, lower, 1, 0)
        query_grad[0, :, columns] = (grad * HD**-0.5).T.astype(BF16)
        key_grad += dot(upper, q, 1, 0) + dot(lower, q, 1, 0)
        value_grad += dot(held, out_grad, 1, 0)
    grads = jnp.concatenate([key_grad * HD**-0.5, value_grad], axis=1).astype(BF16)
    joined[:SEQ] = grads
    shares = jnp.sum(grads.astype(F32) * projected, axis=1, keepdims=True)
    row = jnp.broadcast_to(shares, (SEQ, 128)).T[:EXTRA]
    at_row = lax.broadcasted_iota(jnp.int32, (EXTRA, SEQ), 0)
    terms = jnp.zeros((EXTRA, SEQ), F32)
    for index, term in enumerate(three(row)):
        terms = jnp.where(at_row == index, term.astype(F32), terms)
    joined[SEQ:] = terms.astype(BF16)


def three(value):
    terms = []
    for _ in range(3):
        terms.append(value.astype(BF16))
        value = value - terms[-1].astype(F32)
    return terms


def slab_kernel(where, turned, own, sib, out):
    k = lax.rem(pl.program_id(0) - where[3] + 4, 4)
    for j in range(4):
        term = dot(turned[0, 0, j], own[k, :SEQ], 1, 0).astype(BF16).astype(F32)
        term += dot(turned[0, 1, j], sib[k, :SEQ], 1, 0).astype(BF16).astype(F32)
        out[j] = term.astype(BF16)


def total_kernel(parts, out):
    total = parts[0].astype(F32)
    for k in range(1, 16):
        total += parts[k].astype(F32)
    out[...] = total.astype(BF16)


def spread_kernel(where, keep, sib, inverse, sib_inverse, own_heads, sib_heads, blocks, own_out, sib_out, products):
    @pl.when(pl.program_id(0) == 0)
    def _():
        for s, heads in enumerate((own_heads, sib_heads)):
            rows = [dot(heads[k, SEQ:], jnp.ones((EXTRA, BLOCK), BF16), 0, 0) for k in range(4)]
            products[s] = sum(rows) / D

    for s, heads, states, scale, out in (
        (1, sib_heads, sib, sib_inverse, sib_out),
        (0, own_heads, keep, inverse, own_out),
    ):
        spread = jnp.zeros((SEQ, BLOCK), F32)
        for b in range(4):
            term = dot(heads[lax.rem(b - where[3] + 4, 4), :SEQ], blocks[b, 0], 1, 1)
            spread += term.astype(BF16).astype(F32)
        scaled = states[0, 0].astype(F32) * scale[0]
        out[0] = (scale[0] * (spread - scaled * products[s])).astype(BF16)


def unsplit_kernel(has_old, where, keep, got, *refs):
    out = refs[-1]
    core = where[2]
    for mine in range(2):

        @pl.when(core == mine)
        def _():
            for j in range(4):
                for part, half in ((keep, mine), (got, 1 - mine)):
                    first = (2 * j + half) * BLOCK
                    out[0, :, first : first + BLOCK] = part[j]


def place_kernel(where, *refs):
    out = refs[8]
    for depth in range(2):
        for k in range(2):
            first = pl.multiple_of((where[2] if k == 0 else 1 - where[2]) * BLOCK, BLOCK)
            near, far = refs[4 * depth + k], refs[4 * depth + 2 + k]
            out[depth, pl.ds(first, BLOCK), :] = near[...].astype(F32) + far[...].astype(F32)


TILE = (SEQ, BLOCK)
ANY = pl.BlockSpec(memory_space=pl.ANY)


def shape(dims, dtype):
    return jax.ShapeDtypeStruct(dims, dtype)


def whole(*dims):
    return pl.BlockSpec(dims, lambda *_: (0,) * len(dims))


def layer_of(depth, *dims):
    return pl.BlockSpec((1,) + dims, lambda *_: (depth,) + (0,) * len(dims))


def run(kernel, grid, outs, in_specs, out_specs, args, scratch=(), aliases={}, megaflops=1, scalars=True):
    return pl.pallas_call(
        kernel,
        out_shape=outs,
        grid_spec=pltpu.PrefetchScalarGridSpec(
            num_scalar_prefetch=1 if scalars else 0,
            grid=(grid,),
            in_specs=in_specs,
            out_specs=out_specs,
            scratch_shapes=scratch,
        ),
        input_output_aliases=aliases,
        compiler_params=pltpu.CompilerParams(vmem_limit_bytes=VMEM_BYTES),
        cost_estimate=pl.CostEstimate(flops=megaflops * 10**6, bytes_accessed=6 << 20, transcendentals=0),
    )(*args)


def split(where, hidden):
    parts = pl.BlockSpec((1, 4) + TILE, lambda d, w: (d, 0, 0, 0))
    return run(
        split_kernel,
        2,
        [shape((2, 4) + TILE, BF16)] * 2,
        [pl.BlockSpec((1, SEQ, 2048), lambda d, w: (d, 0, 0))],
        [parts, parts],
        (where, hidden),
    )


def normalize(states):
    pair = pl.BlockSpec((1, 4) + TILE, lambda d: (d, 0, 0, 0))
    scale = pl.BlockSpec((1, SEQ, 1), lambda d: (d, 0, 0))
    out = pl.BlockSpec((1, 2, 4) + TILE, lambda d: (d, 0, 0, 0, 0))
    return run(
        norm_kernel,
        2,
        [shape((2, 2, 4) + TILE, BF16)] * 2,
        [pair, pair, scale, scale],
        [out, out],
        states,
        scalars=False,
    )


def project(depth, side, where, normed, blocks):
    return run(
        project_kernel,
        4,
        shape((4,) + TILE, F32),
        [
            pl.BlockSpec((1, 1, 4) + TILE, lambda k, w: (depth, side, 0, 0, 0)),
            pl.BlockSpec((1, 4) + TILE, lambda k, w: (lax.rem(k + w[3], 4), 0, 0, 0)),
        ],
        pl.BlockSpec((1,) + TILE, lambda k, w: (k, 0, 0)),
        (where, normed, blocks),
        megaflops=537,
    )


def merge(own, got):
    return run(
        merge_kernel,
        1,
        [shape(TILE, F32)] * 4,
        [whole(4, *TILE)] * 2,
        [whole(*TILE)] * 4,
        (own, got),
        scalars=False,
    )


def attend(depth, parts, queries, cotangent, old):
    heads = layer_of(depth, SEQ, GROUP * HD)
    return run(
        functools.partial(attend_kernel, bool(old)),
        1,
        [shape(queries.shape, BF16)] * 2 + [shape((SEQ + EXTRA, BLOCK), BF16)],
        [whole(*TILE)] * 4 + [heads] * 2 + [ANY] * len(old),
        [heads, heads, whole(SEQ + EXTRA, BLOCK)],
        (*parts, queries, cotangent, *old),
        aliases={6: 0, 7: 1} if old else {},
        megaflops=5000,
        scalars=False,
    )


def slab_terms(depth, where, turned, own, sib):
    return run(
        slab_kernel,
        4,
        shape((16,) + TILE, BF16),
        [layer_of(depth, 2, 4, *TILE)] + [whole(4, SEQ + EXTRA, BLOCK)] * 2,
        pl.BlockSpec((4,) + TILE, lambda b, w: (b, 0, 0)),
        (where, turned, own, sib),
        megaflops=1074,
    )


def plane_total(parts):
    return run(
        total_kernel,
        4,
        shape(TILE, BF16),
        [pl.BlockSpec((16, 64, BLOCK), lambda s: (0, s, 0))],
        pl.BlockSpec((64, BLOCK), lambda s: (s, 0)),
        (parts,),
        scalars=False,
    )


def spread_out(depth, where, states, own, sib, blocks):
    state = pl.BlockSpec((1, 1) + TILE, lambda j, w: (depth, j, 0, 0))
    row = pl.BlockSpec((4, 1) + TILE, lambda j, w: (0, j, 0, 0))
    out = pl.BlockSpec((1,) + TILE, lambda j, w: (j, 0, 0))
    return run(
        spread_kernel,
        4,
        [shape((4,) + TILE, BF16)] * 2,
        [state] * 2 + [layer_of(depth, SEQ, 1)] * 2 + [whole(4, SEQ + EXTRA, BLOCK)] * 2 + [row],
        [out, out],
        (where, *states, own, sib, blocks),
        [pltpu.VMEM((2,) + TILE, F32)],
        megaflops=1074,
    )


def unsplit(depth, where, keep, got, dims, old):
    return run(
        functools.partial(unsplit_kernel, bool(old)),
        1,
        shape(dims, BF16),
        [whole(4, *TILE)] * 2 + [ANY] * len(old),
        layer_of(depth, SEQ, 2048),
        (where, keep, got, *old),
        aliases={3: 0} if old else {},
    )


def place(where, quarters):
    return run(
        place_kernel,
        1,
        shape((2, 512, BLOCK), F32),
        [whole(*TILE)] * 8,
        whole(2, 512, BLOCK),
        (where, *quarters),
    )


def shards(hidden, queries, cotangent, slabs):
    layer, dp, high = lax.axis_index("layer"), lax.axis_index("dp"), lax.axis_index("tensor")
    core, low = dp % 2, dp // 2
    where = jnp.stack([layer // 4, layer % 4, core, high, low]).astype(jnp.int32)

    half = lax.dynamic_slice_in_dim(slabs, core * BLOCK, BLOCK, 1)
    owned = shift(half[0], SWAP)
    keep, send = split(where, hidden)
    sib = shift(send, CORE)
    floats = hidden.astype(F32)
    squares = jnp.sum(floats * floats, axis=-1)
    owned = after(owned, send, squares)
    squares = squares + sum(shift(squares, along_high(k)) for k in (1, 2, 3))
    inverse = lax.rsqrt(squares / D + EPSILON)
    states = (keep, sib, inverse[..., None], shift(inverse, CORE)[..., None])
    normed, turned = normalize(states)

    def fetch(sent):
        return lax.all_to_all(sent, "layer", 0, 0, tiled=True)

    def partial(depth, part):
        away = shift(project(depth, 1, where, normed, part), CORE)
        return merge(project(depth, 0, where, normed, part), away)

    def reduce_heads(sums):
        arrived = {k: shift(sums[k], along_high(k)) for k in STEPS}
        return [sums[0]] + [arrived[k] for k in (1, 2, 3)]

    def gather_heads(joined):
        arrived = {k: shift(joined, along_high(-k)) for k in STEPS}
        return jnp.stack([joined] + [arrived[k] for k in (1, 2, 3)])

    def spread(placed):
        return [placed] + [shift(placed, pairs) for pairs in (CORE, LOW, BOTH)]

    sent = jnp.broadcast_to(owned, (16,) + TILE)
    blocks = fetch(sent)
    owned = shift(after(half[1], sent), SWAP)
    sent = jnp.broadcast_to(owned, (16,) + TILE)
    blocks0 = after(blocks, sent).reshape((4, 4) + TILE)
    sums = partial(0, blocks0)
    sent = after(sent, *sums)
    parts = reduce_heads(sums)
    parts, blocks1 = lax.optimization_barrier((parts, fetch(sent)))
    blocks1 = blocks1.reshape((4, 4) + TILE)
    attended, query_grads, joined = attend(0, parts, queries, cotangent, [])
    sums = partial(1, blocks1)

    joined, parts = lax.optimization_barrier((joined, reduce_heads(sums)))
    own0 = gather_heads(joined)
    attended, query_grads, joined = attend(1, parts, queries, cotangent, [attended, query_grads])
    own0, joined = lax.optimization_barrier((own0, joined))
    sib0 = shift(own0, CORE)
    terms0 = slab_terms(0, where, turned, own0, sib0)
    own0, sib0 = after((own0, sib0), terms0)
    terms0 = fetch(terms0)

    own1 = lax.all_gather(joined, "tensor", axis=0)
    in_order = where.at[3].set(0)
    sib1 = shift(own1, CORE)
    terms1 = slab_terms(1, in_order, turned, own1, sib1)
    own1, sib1, own0 = after((own1, sib1, own0), terms1)
    terms1 = fetch(terms1)
    own_out, sib_out = spread_out(0, where, states, own0, sib0, blocks0)
    hidden_grads = unsplit(0, where, own_out, shift(sib_out, CORE), hidden.shape, [])
    own_out, sib_out = spread_out(1, in_order, states, own1, sib1, blocks1)
    hidden_grads = unsplit(1, where, own_out, shift(sib_out, CORE), hidden.shape, [hidden_grads])

    total = after(plane_total(terms0), own_out)
    quarters = spread(shift(total, SWAP))
    total = plane_total(after(terms1, total, hidden_grads))
    quarters += spread(shift(total, SWAP))
    return attended, query_grads, hidden_grads, place(where, quarters)


def solution(mesh):
    tokens = P(None, ("layer", "dp"), "tensor")
    rows = P(None, "layer", "tensor")
    return jax.shard_map(
        shards,
        mesh=mesh,
        in_specs=(tokens, tokens, tokens, rows),
        out_specs=(tokens, tokens, tokens, rows),
        check_vma=False,
    )
```

```python
import functools

import jax
import jax.numpy as jnp
from jax import lax
from jax.experimental import pallas as pl
from jax.experimental.pallas import tpu as pltpu
from jax.sharding import PartitionSpec as P

D = 8192
HD = 128
GROUP = 8
SEQ = 256
EPSILON = 1e-05
BF16 = jnp.bfloat16
F32 = jnp.float32
AXES = ("layer", "dp", "tensor")
BLOCK = 256
VMEM_BYTES = 16 * 1024 * 1024
EXTRA = 16
LOG2E = 1.4426950408889634


def route(move):
    def flat(x, y, low, core, high):
        return ((x * 4 + y) * 4 + low * 2 + core) * 4 + high

    pairs = []
    for x in range(4):
        for y in range(4):
            for low in range(2):
                for core in range(2):
                    for high in range(4):
                        pairs.append((flat(x, y, low, core, high), flat(*move(x, y, low, core, high))))
    return pairs


def along_high(step):
    return route(lambda x, y, low, core, high: (x, y, low, core, (high + step) % 4))


CORE = route(lambda x, y, low, core, high: (x, y, low, 1 - core, high))
LOW = route(lambda x, y, low, core, high: (x, y, 1 - low, core, high))
BOTH = route(lambda x, y, low, core, high: (x, y, 1 - low, 1 - core, high))
SWAP = route(lambda x, y, low, core, high: (high, y, low, core, x))
STEPS = (1, 3, 2)


def shift(value, pairs):
    return lax.ppermute(value, AXES, pairs)


def after(value, *others):
    return lax.optimization_barrier((value, others))[0]


def dot(a, b, ca, cb):
    return lax.dot_general(a, b, (((ca,), (cb,)), ((), ())), preferred_element_type=F32)


def split_kernel(where, hidden, keep, send):
    core = where[2]
    for mine in range(2):

        @pl.when(core == mine)
        def _():
            for j in range(4):
                for out, half in ((keep, mine), (send, 1 - mine)):
                    first = (2 * j + half) * BLOCK
                    out[0, j] = hidden[0, :, first : first + BLOCK]


def norm_kernel(keep, sib, inverse, sib_inverse, normed, turned):
    for s, states, scale in ((0, keep, inverse), (1, sib, sib_inverse)):
        for j in range(4):
            part = (states[0, j].astype(F32) * scale[0]).astype(BF16)
            normed[0, s, j] = part
            turned[0, s, j] = part.T


def project_kernel(where, normed, blocks, out):
    out[0] = sum(dot(normed[0, 0, j], blocks[0, j], 1, 0) for j in range(4))


def merge_kernel(own, got, *outs):
    for k in range(4):
        outs[k][...] = own[k] + got[k]


def attend_kernel(has_old, *refs):
    parts, refs = refs[:4], refs[4:]
    query, cotangent = refs[:2]
    refs = refs[4:] if has_old else refs[2:]
    attended, query_grad, joined = refs
    projected = (parts[0][...] + parts[1][...]) + (parts[2][...] + parts[3][...])
    rounded = projected.astype(BF16)
    k, v = rounded[:, :HD], rounded[:, HD:]
    kt, vt = k.T, v.T
    to = lax.broadcasted_iota(jnp.int32, (SEQ, SEQ), 0)
    at = lax.broadcasted_iota(jnp.int32, (SEQ, SEQ), 1)
    key_grad = jnp.zeros((SEQ, HD), F32)
    value_grad = jnp.zeros((SEQ, HD), F32)
    for head in range(GROUP):
        columns = slice(head * HD, (head + 1) * HD)
        q, out_grad = query[0, :, columns], cotangent[0, :, columns]
        scores = jnp.where(at >= to, dot(k, q, 1, 1), -1e30)
        weights = jnp.exp2((scores - jnp.max(scores, axis=0, keepdims=True)) * (HD**-0.5 * LOG2E))
        weights = weights * (1.0 / jnp.sum(weights, axis=0, keepdims=True))
        held = weights.astype(BF16)
        attended[0, :, columns] = dot(vt, held, 1, 0).T.astype(BF16)
        weight_grad = dot(v, out_grad, 1, 1).astype(BF16).astype(F32)
        mean = jnp.sum(weights * weight_grad, axis=0, keepdims=True)
        score_grad = weights * (weight_grad - mean)
        upper = score_grad.astype(BF16)
        lower = (score_grad - upper.astype(F32)).astype(BF16)
        grad = dot(kt, upper, 1, 0) + dot(kt, lower, 1, 0)
        query_grad[0, :, columns] = (grad * HD**-0.5).T.astype(BF16)
        key_grad += dot(upper, q, 1, 0) + dot(lower, q, 1, 0)
        value_grad += dot(held, out_grad, 1, 0)
    grads = jnp.concatenate([key_grad * HD**-0.5, value_grad], axis=1).astype(BF16)
    joined[:SEQ] = grads
    shares = jnp.sum(grads.astype(F32) * projected, axis=1, keepdims=True)
    row = jnp.broadcast_to(shares, (SEQ, 128)).T[:EXTRA]
    at_row = lax.broadcasted_iota(jnp.int32, (EXTRA, SEQ), 0)
    terms = jnp.zeros((EXTRA, SEQ), F32)
    for index, term in enumerate(three(row)):
        terms = jnp.where(at_row == index, term.astype(F32), terms)
    joined[SEQ:] = terms.astype(BF16)


def three(value):
    terms = []
    for _ in range(3):
        terms.append(value.astype(BF16))
        value = value - terms[-1].astype(F32)
    return terms


def slab_kernel(where, turned, own, sib, out):
    k = lax.rem(pl.program_id(0) - where[3] + 4, 4)
    for j in range(4):
        term = dot(turned[0, 0, j], own[k, :SEQ], 1, 0).astype(BF16).astype(F32)
        term += dot(turned[0, 1, j], sib[k, :SEQ], 1, 0).astype(BF16).astype(F32)
        out[j] = term.astype(BF16)


def total_kernel(parts, out):
    total = parts[0].astype(F32)
    for k in range(1, 16):
        total += parts[k].astype(F32)
    out[...] = total.astype(BF16)


def spread_kernel(where, keep, sib, inverse, sib_inverse, own_heads, sib_heads, blocks, own_out, sib_out, products):
    @pl.when(pl.program_id(0) == 0)
    def _():
        for s, heads in enumerate((own_heads, sib_heads)):
            rows = [dot(heads[k, SEQ:], jnp.ones((EXTRA, BLOCK), BF16), 0, 0) for k in range(4)]
            products[s] = sum(rows) / D

    for s, heads, states, scale, out in (
        (1, sib_heads, sib, sib_inverse, sib_out),
        (0, own_heads, keep, inverse, own_out),
    ):
        spread = jnp.zeros((SEQ, BLOCK), F32)
        for b in range(4):
            term = dot(heads[lax.rem(b - where[3] + 4, 4), :SEQ], blocks[b, 0], 1, 1)
            spread += term.astype(BF16).astype(F32)
        scaled = states[0, 0].astype(F32) * scale[0]
        out[0] = (scale[0] * (spread - scaled * products[s])).astype(BF16)


def unsplit_kernel(has_old, where, keep, got, *refs):
    out = refs[-1]
    core = where[2]
    for mine in range(2):

        @pl.when(core == mine)
        def _():
            for j in range(4):
                for part, half in ((keep, mine), (got, 1 - mine)):
                    first = (2 * j + half) * BLOCK
                    out[0, :, first : first + BLOCK] = part[j]


def place_kernel(where, *refs):
    out = refs[8]
    for depth in range(2):
        for k in range(2):
            first = pl.multiple_of((where[2] if k == 0 else 1 - where[2]) * BLOCK, BLOCK)
            near, far = refs[4 * depth + k], refs[4 * depth + 2 + k]
            out[depth, pl.ds(first, BLOCK), :] = near[...].astype(F32) + far[...].astype(F32)


TILE = (SEQ, BLOCK)
ANY = pl.BlockSpec(memory_space=pl.ANY)


def shape(dims, dtype):
    return jax.ShapeDtypeStruct(dims, dtype)


def whole(*dims):
    return pl.BlockSpec(dims, lambda *_: (0,) * len(dims))


def layer_of(depth, *dims):
    return pl.BlockSpec((1,) + dims, lambda *_: (depth,) + (0,) * len(dims))


def run(kernel, grid, outs, in_specs, out_specs, args, scratch=(), aliases={}, megaflops=1, scalars=True):
    return pl.pallas_call(
        kernel,
        out_shape=outs,
        grid_spec=pltpu.PrefetchScalarGridSpec(
            num_scalar_prefetch=1 if scalars else 0,
            grid=(grid,),
            in_specs=in_specs,
            out_specs=out_specs,
            scratch_shapes=scratch,
        ),
        input_output_aliases=aliases,
        compiler_params=pltpu.CompilerParams(vmem_limit_bytes=VMEM_BYTES),
        cost_estimate=pl.CostEstimate(flops=megaflops * 10**6, bytes_accessed=6 << 20, transcendentals=0),
    )(*args)


def split(where, hidden):
    parts = pl.BlockSpec((1, 4) + TILE, lambda d, w: (d, 0, 0, 0))
    return run(
        split_kernel,
        2,
        [shape((2, 4) + TILE, BF16)] * 2,
        [pl.BlockSpec((1, SEQ, 2048), lambda d, w: (d, 0, 0))],
        [parts, parts],
        (where, hidden),
    )


def normalize(states):
    pair = pl.BlockSpec((1, 4) + TILE, lambda d: (d, 0, 0, 0))
    scale = pl.BlockSpec((1, SEQ, 1), lambda d: (d, 0, 0))
    out = pl.BlockSpec((1, 2, 4) + TILE, lambda d: (d, 0, 0, 0, 0))
    return run(
        norm_kernel,
        2,
        [shape((2, 2, 4) + TILE, BF16)] * 2,
        [pair, pair, scale, scale],
        [out, out],
        states,
        scalars=False,
    )


def project(depth, side, where, normed, blocks):
    return run(
        project_kernel,
        4,
        shape((4,) + TILE, F32),
        [
            pl.BlockSpec((1, 1, 4) + TILE, lambda k, w: (depth, side, 0, 0, 0)),
            pl.BlockSpec((1, 4) + TILE, lambda k, w: (lax.rem(k + w[3], 4), 0, 0, 0)),
        ],
        pl.BlockSpec((1,) + TILE, lambda k, w: (k, 0, 0)),
        (where, normed, blocks),
        megaflops=537,
    )


def merge(own, got):
    return run(
        merge_kernel,
        1,
        [shape(TILE, F32)] * 4,
        [whole(4, *TILE)] * 2,
        [whole(*TILE)] * 4,
        (own, got),
        scalars=False,
    )


def attend(depth, parts, queries, cotangent, old):
    heads = layer_of(depth, SEQ, GROUP * HD)
    return run(
        functools.partial(attend_kernel, bool(old)),
        1,
        [shape(queries.shape, BF16)] * 2 + [shape((SEQ + EXTRA, BLOCK), BF16)],
        [whole(*TILE)] * 4 + [heads] * 2 + [ANY] * len(old),
        [heads, heads, whole(SEQ + EXTRA, BLOCK)],
        (*parts, queries, cotangent, *old),
        aliases={6: 0, 7: 1} if old else {},
        megaflops=5000,
        scalars=False,
    )


def slab_terms(depth, where, turned, own, sib):
    return run(
        slab_kernel,
        4,
        shape((16,) + TILE, BF16),
        [layer_of(depth, 2, 4, *TILE)] + [whole(4, SEQ + EXTRA, BLOCK)] * 2,
        pl.BlockSpec((4,) + TILE, lambda b, w: (b, 0, 0)),
        (where, turned, own, sib),
        megaflops=1074,
    )


def plane_total(parts):
    return run(
        total_kernel,
        4,
        shape(TILE, BF16),
        [pl.BlockSpec((16, 64, BLOCK), lambda s: (0, s, 0))],
        pl.BlockSpec((64, BLOCK), lambda s: (s, 0)),
        (parts,),
        scalars=False,
    )


def spread_out(depth, where, states, own, sib, blocks):
    state = pl.BlockSpec((1, 1) + TILE, lambda j, w: (depth, j, 0, 0))
    row = pl.BlockSpec((4, 1) + TILE, lambda j, w: (0, j, 0, 0))
    out = pl.BlockSpec((1,) + TILE, lambda j, w: (j, 0, 0))
    return run(
        spread_kernel,
        4,
        [shape((4,) + TILE, BF16)] * 2,
        [state] * 2 + [layer_of(depth, SEQ, 1)] * 2 + [whole(4, SEQ + EXTRA, BLOCK)] * 2 + [row],
        [out, out],
        (where, *states, own, sib, blocks),
        [pltpu.VMEM((2,) + TILE, F32)],
        megaflops=1074,
    )


def unsplit(depth, where, keep, got, dims, old):
    return run(
        functools.partial(unsplit_kernel, bool(old)),
        1,
        shape(dims, BF16),
        [whole(4, *TILE)] * 2 + [ANY] * len(old),
        layer_of(depth, SEQ, 2048),
        (where, keep, got, *old),
        aliases={3: 0} if old else {},
    )


def place(where, quarters):
    return run(
        place_kernel,
        1,
        shape((2, 512, BLOCK), F32),
        [whole(*TILE)] * 8,
        whole(2, 512, BLOCK),
        (where, *quarters),
    )


def shards(hidden, queries, cotangent, slabs):
    layer, dp, high = lax.axis_index("layer"), lax.axis_index("dp"), lax.axis_index("tensor")
    core, low = dp % 2, dp // 2
    where = jnp.stack([layer // 4, layer % 4, core, high, low]).astype(jnp.int32)

    half = lax.dynamic_slice_in_dim(slabs, core * BLOCK, BLOCK, 1)
    owned = shift(half[0], SWAP)
    keep, send = split(where, hidden)
    sib = shift(send, CORE)
    floats = hidden.astype(F32)
    squares = jnp.sum(floats * floats, axis=-1)
    owned = after(owned, send, squares)
    squares = squares + sum(shift(squares, along_high(k)) for k in (1, 2, 3))
    inverse = lax.rsqrt(squares / D + EPSILON)
    states = (keep, sib, inverse[..., None], shift(inverse, CORE)[..., None])
    normed, turned = normalize(states)

    def fetch(sent):
        return lax.all_to_all(sent, "layer", 0, 0, tiled=True)

    def partial(depth, part):
        away = shift(project(depth, 1, where, normed, part), CORE)
        return merge(project(depth, 0, where, normed, part), away)

    def reduce_heads(sums):
        arrived = {k: shift(sums[k], along_high(k)) for k in STEPS}
        return [sums[0]] + [arrived[k] for k in (1, 2, 3)]

    def spread(placed):
        return [placed] + [shift(placed, pairs) for pairs in (CORE, LOW, BOTH)]

    sent = jnp.broadcast_to(owned, (16,) + TILE)
    blocks = fetch(sent)
    owned = shift(after(half[1], sent), SWAP)
    sent = jnp.broadcast_to(owned, (16,) + TILE)
    blocks0 = after(blocks, sent).reshape((4, 4) + TILE)
    sums = partial(0, blocks0)
    sent = after(sent, *sums)
    parts = reduce_heads(sums)
    parts, blocks1 = lax.optimization_barrier((parts, fetch(sent)))
    blocks1 = blocks1.reshape((4, 4) + TILE)
    attended, query_grads, joined = attend(0, parts, queries, cotangent, [])
    sums = partial(1, blocks1)

    joined, parts = lax.optimization_barrier((joined, reduce_heads(sums)))
    own0 = lax.all_gather(joined, "tensor", axis=0)
    in_order = where.at[3].set(0)
    sib0 = shift(own0, CORE)
    terms0 = slab_terms(0, in_order, turned, own0, sib0)
    own0, sib0, parts = after((own0, sib0, parts), terms0)
    terms0 = fetch(terms0)
    attended, query_grads, joined = attend(1, parts, queries, cotangent, [attended, query_grads])

    own1 = lax.all_gather(joined, "tensor", axis=0)
    sib1 = shift(own1, CORE)
    terms1 = slab_terms(1, in_order, turned, own1, sib1)
    own1, sib1, own0 = after((own1, sib1, own0), terms1)
    terms1 = fetch(terms1)
    own_out, sib_out = spread_out(0, in_order, states, own0, sib0, blocks0)
    hidden_grads = unsplit(0, where, own_out, shift(sib_out, CORE), hidden.shape, [])
    own_out, sib_out = spread_out(1, in_order, states, own1, sib1, blocks1)
    hidden_grads = unsplit(1, where, own_out, shift(sib_out, CORE), hidden.shape, [hidden_grads])

    total = after(plane_total(terms0), own_out)
    quarters = spread(shift(total, SWAP))
    total = plane_total(after(terms1, total, hidden_grads))
    quarters += spread(shift(total, SWAP))
    return attended, query_grads, hidden_grads, place(where, quarters)


def solution(mesh):
    tokens = P(None, ("layer", "dp"), "tensor")
    rows = P(None, "layer", "tensor")
    return jax.shard_map(
        shards,
        mesh=mesh,
        in_specs=(tokens, tokens, tokens, rows),
        out_specs=(tokens, tokens, tokens, rows),
        check_vma=False,
    )
```
